32 devices in a mesh: groups: 2 (over x), dp: 4 (over z), fsdp: 4 (over y, core).
Axes of the slice: x: 2, y: 2, z: 4, core: 2. Of those that a mesh axis runs over, the one named last changes fastest.
Arguments:
- acts: bfloat16 [7168, 8192], P(('groups', 'dp'), 'fsdp'), parts along dimension 0, may hold values from -6 to 6
- out_grad: bfloat16 [7168, 8192], P(('groups', 'dp'), 'fsdp'), parts along dimension 0, may hold values from -6 to 6
- gate_pre: bfloat16 [7168, 14336], P(('groups', 'dp'), 'fsdp'), parts along dimension 0, may hold values from -8 to 8
- down_weight: bfloat16 [14336, 8192], P('fsdp', 'dp'), may hold values from -0.0625 to 0.0625
- proj_in: bfloat16 [64, 8192], P(None, 'fsdp'), may hold values from -0.0625 to 0.0625
- proj_out: bfloat16 [64, 14336], P(None, 'fsdp'), may hold values from -0.046875 to 0.046875
- lengths: int32 [8, 16], P(('groups', 'dp')), parts along dimension 0, may hold values from 1 to 112, 896 in all within a row
Outputs:
- fisher: float32 [8192, 4096], P(('groups', 'dp', 'fsdp')), parts along dimension 0
The draws below stay inside these ranges and needn't reach their ends.
There are 2 independent parts, one for each index of `groups`. The reference program is written for one: setup_inputs(seed, part) draws one part's arguments, and reference() takes and returns one part's arrays. A program takes and returns all parts, laid end to end along the dimension named above; an argument that names none is the same for every part. Nothing has to cross between parts.
Inputs may be any that keep to these rules, and one draw needn't show every extreme that they name: `lengths`: every row sums to 896, and some example of every row holds exactly 112 tokens.
All inputs are finite; a program needn't handle non-finite values.
Results may differ from the reference program's by a relative error of at most 0.0041.
Values may be sent and summed in bfloat16 or wider, within the bound.
No kernel may reach another device: no remote copies, remote signals or barrier semaphores. Data moves between devices by JAX's collectives and lax.ppermute only.
A program may use at most 256 MiB of HBM per device.

```python
import math
import jax
import jax.numpy as jnp
import numpy as np
from jax import lax

D = 8192
FF = 14336
RANK_IN = 64
RANK_OUT = 64
TOK_DEV = 896
EX_DEV = 16
MOST = 112
TOKENS = 3584
EXAMPLES = 64
PROJ = 4096
N_DP = 4


def levels(rng, extent, shards, least, high):
    level = 1.0
    for axis_at, shards_of in shards:
        draws = jax.random.uniform(jax.random.fold_in(jax.random.fold_in(rng, 6), axis_at), (shards_of,), jnp.float32, least / len(shards), high / len(shards))
        level = level * jnp.repeat(jnp.exp(draws), extent[axis_at] // shards_of).reshape((-1,) + (1,) * (len(extent) - 1 - axis_at))
    return level


def split_up(count, total, most, skew):
    portions = [(1 << 20) // math.isqrt(grade ** skew) + 1 for grade in range(2, count + 1)]
    surplus, given = total - most - (count - 1), [1] * (count - 1)
    while surplus > 0:
        movable = [i for i in range(count - 1) if given[i] < most]
        whole, budget = sum([portions[i] for i in movable]), surplus
        for i in movable:
            extra = min(most - given[i], max(1, budget * portions[i] // whole), surplus)
            given[i] = given[i] + extra
            surplus = surplus - extra
    return np.array([most] + given)


def ragged_sizes(rng, amount, total, limit, slope):
    if amount == 2:
        one = jax.random.randint(rng, (), max(1, total - limit), min(limit, total - 1) + 1)
        return jnp.stack([one, total - one])
    sizes = jnp.asarray(split_up(amount, total, limit, slope), jnp.int32)
    pairs = (amount - 1) // 2
    donor, receiver = sizes[1:1 + 2 * pairs:2], sizes[2:2 + 2 * pairs:2]
    room = jnp.minimum(donor - 1, limit - receiver)
    shifted = jax.random.randint(jax.random.fold_in(rng, 1), (pairs,), 0, 1 << 20) % (room + 1)
    sizes = sizes.at[1:1 + 2 * pairs:2].set(donor - shifted).at[2:2 + 2 * pairs:2].set(receiver + shifted)
    return sizes[jax.random.permutation(jax.random.fold_in(rng, 2), amount)]


def noise(key, extent, deviation, most, cuts=(), kind=jnp.bfloat16):
    entries = jax.random.normal(key, extent, jnp.float32) * deviation
    if len(cuts) > 0:
        entries = levels(key, extent, cuts, -0.22, 0.18) * entries
    return jnp.clip(entries, min=-most, max=most).astype(kind)


def setup_inputs(seed: int = 0, part: int = 0) -> dict:
    seeds = jax.random.split(jax.random.key(seed), 8)
    own_keys = jax.random.split(jax.random.fold_in(seeds[7], part), 8)
    acts = noise(own_keys[0], (TOKENS, D), 1.0, 6.0, ((0, 4), (1, 4)))
    out_grad = noise(own_keys[1], (TOKENS, D), 1.0, 6.0, ((0, 4), (1, 4)))
    gate_pre = noise(own_keys[2], (TOKENS, FF), 1.5, 8.0, ((0, 4), (1, 4)))
    down_weight = noise(seeds[3], (FF, D), D ** -0.5, 0.0625, ((0, 4), (1, 4)))
    proj_in = noise(seeds[4], (RANK_IN, D), D ** -0.5, 0.0625, ((1, 4),))
    proj_out = noise(seeds[5], (RANK_OUT, FF), FF ** -0.5, 0.046875, ((1, 4),))
    lengths = jax.vmap(lambda own: ragged_sizes(own, EX_DEV, TOK_DEV, MOST, 2))(jax.random.split(own_keys[6], N_DP)).reshape((N_DP, EX_DEV)).astype(jnp.int32)
    return dict(acts=acts, out_grad=out_grad, gate_pre=gate_pre, down_weight=down_weight, proj_in=proj_in, proj_out=proj_out, lengths=lengths)


def reference(acts, out_grad, gate_pre, down_weight, proj_in, proj_out, lengths):
    def one_row(inputs):
        row_acts, row_grad, row_gate, row_counts = inputs
        factors_in = lax.dot_general(row_acts, proj_in, (((1,), (1,)), ((), ())), preferred_element_type=jnp.float32)
        upstream = lax.dot_general(row_grad, down_weight, (((1,), (1,)), ((), ())), preferred_element_type=jnp.float32)
        up_grad = (upstream * jax.nn.silu(row_gate.astype(jnp.float32))).astype(jnp.bfloat16)
        factors_out = lax.dot_general(up_grad, proj_out, (((1,), (1,)), ((), ())), preferred_element_type=jnp.float32)
        stop_at = jnp.cumsum(row_counts, dtype=jnp.int32)
        starts = stop_at - row_counts
        position = jnp.arange(TOK_DEV, dtype=jnp.int32)
        member = ((position[None, :] >= starts[:, None]) & (position[None, :] < stop_at[:, None])).astype(jnp.float32)
        weighted = member[:, :, None] * factors_in[None, :, :]
        outer = jnp.einsum("eti,tj->eij", weighted, factors_out, precision=lax.Precision.HIGHEST)
        return outer.reshape(EX_DEV, PROJ)

    example_grads = lax.map(one_row, (acts.reshape(N_DP, TOK_DEV, D), out_grad.reshape(N_DP, TOK_DEV, D), gate_pre.reshape(N_DP, TOK_DEV, FF), lengths))
    example_grads = example_grads.reshape(EXAMPLES, PROJ)
    fisher = jnp.dot(example_grads.T, example_grads, precision=lax.Precision.HIGHEST, preferred_element_type=jnp.float32)
    return fisher / EXAMPLES
```

```python
import functools

import jax
import jax.numpy as jnp
from jax import lax
from jax.experimental import pallas as pl
from jax.experimental.pallas import tpu as pltpu
from jax.sharding import PartitionSpec as P

MATES = [(0, 1), (1, 0), (2, 3), (3, 2)]
ACROSS = [(1, 2), (2, 1)]
OUTWARD = [(1, 0), (2, 3)]
INWARD = [(0, 1), (3, 2)]
CHUNK = 256
VMEM_LIMIT = 58 * 1024 * 1024


def dot_nt(left, right):
    return lax.dot_general(left, right, (((1,), (1,)), ((), ())), preferred_element_type=jnp.float32)


def early_kernel(place, grad_ref, own_ref, mate_ref, near_ref, part_ref):
    step = pl.program_id(1)

    @pl.when(step == 0)
    def _():
        part_ref[...] = dot_nt(grad_ref[0], own_ref[...])

    @pl.when(step == 1)
    def _():
        part_ref[...] += dot_nt(grad_ref[0], mate_ref[...])

    @pl.when(step == 2)
    def _():
        part_ref[...] += dot_nt(grad_ref[0], near_ref[...])


def early_part(place, grads, down_weight, mate_weight, near_weight):
    hidden, width = mate_weight.shape
    tokens_dev = grads.shape[1]
    tile = tokens_dev // 2
    tiles = 2 * tokens_dev // tile
    per = tokens_dev // tile
    return pl.pallas_call(
        early_kernel,
        grid_spec=pltpu.PrefetchScalarGridSpec(
            num_scalar_prefetch=1,
            grid=(tiles, 3),
            in_specs=[
                pl.BlockSpec(
                    (1, tile, width),
                    lambda i, k, place: ((i // per ^ place[0]) * 4 + place[1 + k], i % per, 0),
                ),
                pl.BlockSpec((hidden, width), lambda i, k, place: (place[0], 0), pipeline_mode=pl.Buffered(1)),
                pl.BlockSpec((hidden, width), lambda i, k, place: (0, 0), pipeline_mode=pl.Buffered(1)),
                pl.BlockSpec((hidden, width), lambda i, k, place: (0, 0), pipeline_mode=pl.Buffered(1)),
            ],
            out_specs=pl.BlockSpec((tile, hidden), lambda i, k, place: (i, 0)),
        ),
        out_shape=jax.ShapeDtypeStruct((2 * tokens_dev, hidden), jnp.float32),
        compiler_params=pltpu.CompilerParams(vmem_limit_bytes=VMEM_LIMIT),
        cost_estimate=pl.CostEstimate(
            flops=2 * 2 * tokens_dev * hidden * width * 3,
            bytes_accessed=2 * 2 * tokens_dev * width * 3 + 6 * hidden * width + 8 * tokens_dev * hidden,
            transcendentals=0,
        ),
        name="early_part",
    )(place, grads, down_weight, mate_weight, near_weight)


def late_kernel(
    place, part_ref, grad_ref, far_ref, out_ref, gate_ref, guest_grad_ref, guest_gate_ref, proj_ref, sum_ref, new_ref
):
    inner = place[5] == 1
    far = far_ref[...]
    weight = jnp.where(inner, far, out_ref[...])
    rank = proj_ref.shape[0]

    def project(upstream, gate, exact):
        gate = gate.astype(jnp.float32)
        up_grad = upstream * (gate / (1.0 + jnp.exp(-gate)))
        high = up_grad.astype(jnp.bfloat16)
        low = jnp.where(exact, 0.0, up_grad - high.astype(jnp.float32)).astype(jnp.bfloat16)
        return dot_nt(high, proj_ref[...]) + dot_nt(low, proj_ref[...])

    upstream = part_ref[...] + dot_nt(grad_ref[0], weight)
    new_ref[:, :rank] = sum_ref[:, :rank] + project(upstream, gate_ref[...], inner)
    guest = dot_nt(guest_grad_ref[0], far)
    new_ref[:, rank:] = sum_ref[:, rank:] + project(guest, guest_gate_ref[...], False)


def late_part(place, chunk, part, grads, far, out, gates, guest_grads, guest_gates, proj_out, sums):
    tokens_dev, width = grads.shape[1:]
    hidden = part.shape[1]
    tile = tokens_dev // 2
    per = tokens_dev // tile
    wide = far.shape[0]
    count = hidden // wide
    rank = proj_out.shape[0]
    row = lambda i, place: (i, 0)
    return pl.pallas_call(
        late_kernel,
        grid_spec=pltpu.PrefetchScalarGridSpec(
            num_scalar_prefetch=1,
            grid=(2 * per,),
            in_specs=[
                pl.BlockSpec((tile, wide), lambda i, place: (i, chunk)),
                pl.BlockSpec(
                    (1, tile, width), lambda i, place: ((i // per ^ place[0]) * 4 + place[4], i % per, 0)
                ),
                pl.BlockSpec((wide, width), lambda i, place: (0, 0)),
                pl.BlockSpec((wide, width), lambda i, place: (0, 0)),
                pl.BlockSpec((tile, wide), lambda i, place: (i, chunk)),
                pl.BlockSpec((1, tile, width), lambda i, place: (i // per ^ place[0], i % per, 0)),
                pl.BlockSpec((tile, wide), row),
                pl.BlockSpec((rank, wide), lambda i, place: (0, place[0] * count + chunk)),
                pl.BlockSpec((tile, 2 * rank), row),
            ],
            out_specs=pl.BlockSpec((tile, 2 * rank), row),
        ),
        out_shape=jax.ShapeDtypeStruct(sums.shape, jnp.float32),
        input_output_aliases={9: 0},
        compiler_params=pltpu.CompilerParams(vmem_limit_bytes=VMEM_LIMIT),
        cost_estimate=pl.CostEstimate(
            flops=2 * 4 * tokens_dev * wide * (width + 2 * rank),
            bytes_accessed=8 * tokens_dev * width + 4 * wide * width + 16 * tokens_dev * wide,
            transcendentals=4 * tokens_dev * wide,
        ),
        name="late_part",
    )(place, part, grads, far, out, gates, guest_grads, guest_gates, proj_out, sums)


def example_sums(counts, factors_in, factors_out):
    tok_rows = factors_in.shape[0]
    stop_at = jnp.cumsum(counts, dtype=jnp.int32)
    starts = stop_at - counts
    position = jnp.arange(tok_rows, dtype=jnp.int32)
    member = (
        (position[None, :] >= starts[:, None]) & (position[None, :] < stop_at[:, None])
    ).astype(jnp.float32)
    weighted = member[:, :, None] * factors_in[None, :, :]
    return jnp.einsum(
        "eti,tj->eij", weighted, factors_out, precision=lax.Precision.HIGHEST
    ).reshape(counts.shape[0], -1)


def own_fisher(example_grads):
    every = lax.all_gather(example_grads, "dp", axis=0, tiled=True)
    fsdp_count = lax.axis_size("fsdp")
    own_rows = every.shape[1] // (lax.axis_size("dp") * fsdp_count)
    block = lax.axis_index("dp") * fsdp_count + lax.axis_index("fsdp")
    picked = lax.dynamic_slice_in_dim(every, block * own_rows, own_rows, 1)
    return lax.dot_general(
        picked * (1.0 / every.shape[0]),
        every,
        (((0,), (0,)), ((), ())),
        precision=lax.Precision.HIGHEST,
        preferred_element_type=jnp.float32,
    )


def line_plan(acts, out_grad, gate_pre, down_weight, proj_in, proj_out, lengths):
    x, z, column = lax.axis_index("groups"), lax.axis_index("dp"), lax.axis_index("fsdp")
    inner = (z == 1) | (z == 2)
    near_block, far_block = jnp.where(z < 2, 2, 1), jnp.where(z < 2, 3, 0)
    place = jnp.stack(
        [x, z, z ^ 1, near_block, jnp.where(inner, far_block, near_block), inner.astype(jnp.int32)]
    ).astype(jnp.int32)
    tokens_dev, width = out_grad.shape
    hidden = down_weight.shape[0] // 2
    rank = proj_out.shape[0]

    own_weight = lax.dynamic_slice_in_dim(down_weight, x * hidden, hidden, 0)
    mate_weight = lax.ppermute(own_weight, "dp", MATES)
    near_weight = lax.ppermute(own_weight, "dp", ACROSS)
    grads = lax.all_gather(out_grad, ("groups", "fsdp"), axis=0)
    gate_self = lax.dynamic_slice_in_dim(gate_pre, x * hidden, hidden, 1)
    gate_other = lax.dynamic_slice_in_dim(gate_pre, (1 - x) * hidden, hidden, 1)
    gates = jnp.concatenate([gate_self, lax.ppermute(gate_other, "groups", [(0, 1), (1, 0)])])
    factors_in = lax.psum(dot_nt(acts, proj_in), "fsdp")

    mate_weight, near_weight, gates, grads = lax.optimization_barrier((mate_weight, near_weight, gates, grads))
    piece_rows = tokens_dev // lax.axis_size("fsdp")
    piece = lax.dynamic_slice(
        grads, (x * 4 + far_block, column * piece_rows, 0), (1, piece_rows, width)
    )[0]
    piece = lax.ppermute(piece, "dp", INWARD)
    guest_grads = lax.all_gather(piece, ("groups", "fsdp"), axis=0, tiled=True).reshape(2, tokens_dev, width)
    part = early_part(place, grads, down_weight, mate_weight, near_weight)
    sums = jnp.zeros((2 * tokens_dev, 2 * rank), jnp.float32)
    for chunk in range(hidden // CHUNK):
        rows = slice(chunk * CHUNK, (chunk + 1) * CHUNK)
        far = lax.ppermute(mate_weight[rows], "dp", ACROSS)
        out = lax.ppermute(near_weight[rows], "dp", OUTWARD)
        guest_gates = lax.ppermute(gates[:, rows], "dp", INWARD)
        sums = late_part(place, chunk, part, grads, far, out, gates, guest_grads, guest_gates, proj_out, sums)

    mine = sums[:, :rank] + lax.ppermute(sums[:, rank:], "dp", OUTWARD)
    mine = mine[:tokens_dev] + lax.ppermute(mine[tokens_dev:], "groups", [(0, 1), (1, 0)])
    factors_out = lax.psum(mine, "fsdp")
    return own_fisher(example_sums(lengths[0], factors_in, factors_out))


def ring_plan(acts, out_grad, gate_pre, down_weight, proj_in, proj_out, lengths):
    full_grad = lax.all_gather(out_grad, "fsdp", axis=1, tiled=True)
    upstream = dot_nt(full_grad, lax.all_gather(down_weight, "dp", axis=1, tiled=True))
    up_grad = (upstream * jax.nn.silu(gate_pre.astype(jnp.float32))).astype(jnp.bfloat16)
    rank_in = proj_in.shape[0]
    joined = lax.psum(jnp.concatenate([dot_nt(acts, proj_in), dot_nt(up_grad, proj_out)], axis=1), "fsdp")
    return own_fisher(example_sums(lengths[0], joined[:, :rank_in], joined[:, rank_in:]))


def solution(mesh):
    placed = (
        P(("groups", "dp"), "fsdp"),
        P(("groups", "dp"), "fsdp"),
        P(("groups", "dp"), "fsdp"),
        P("fsdp", "dp"),
        P(None, "fsdp"),
        P(None, "fsdp"),
        P(("groups", "dp"), None),
    )
    line = (mesh.shape["groups"], mesh.shape["dp"], mesh.shape["fsdp"]) == (2, 4, 4)
    return jax.shard_map(
        line_plan if line else ring_plan,
        mesh=mesh,
        in_specs=placed,
        out_specs=P(("groups", "dp", "fsdp"), None),
        check_vma=False,
    )
```

```python
import functools

import jax
import jax.numpy as jnp
from jax import lax
from jax.experimental import pallas as pl
from jax.experimental.pallas import tpu as pltpu
from jax.sharding import PartitionSpec as P

MATES = [(0, 1), (1, 0), (2, 3), (3, 2)]
ACROSS = [(1, 2), (2, 1)]
OUTWARD = [(1, 0), (2, 3)]
INWARD = [(0, 1), (3, 2)]
SWAP = [(0, 1), (1, 0)]
UNIT = 256
FIRST_UNITS = 4
LATE = ((4, (1, 3)), (2, (2,)), (1, (1,)))
EARLY_COST = 2 * 10**7
LATE_COST = 1 << 20
VMEM_LIMIT = 58 * 1024 * 1024


def dot_nt(left, right):
    return lax.dot_general(left, right, (((1,), (1,)), ((), ())), preferred_element_type=jnp.float32)


def early_kernel(place, grad_ref, own_ref, mate_ref, near_ref, part_ref):
    step = pl.program_id(1)

    @pl.when(step == 0)
    def _():
        part_ref[...] = dot_nt(grad_ref[0], own_ref[...])

    @pl.when(step == 1)
    def _():
        part_ref[...] += dot_nt(grad_ref[0], mate_ref[...])

    @pl.when(step == 2)
    def _():
        part_ref[...] += dot_nt(grad_ref[0], near_ref[...])


def early_part(place, grads, own, mate, near):
    hidden, width = own.shape
    tokens_dev = grads.shape[1]
    tile = tokens_dev // 2
    whole = pl.BlockSpec((hidden, width), lambda i, k, place: (0, 0), pipeline_mode=pl.Buffered(1))
    return pl.pallas_call(
        early_kernel,
        grid_spec=pltpu.PrefetchScalarGridSpec(
            num_scalar_prefetch=1,
            grid=(tokens_dev // tile, 3),
            in_specs=[pl.BlockSpec((1, tile, width), lambda i, k, place: (place[1 + k], i, 0)), whole, whole, whole],
            out_specs=pl.BlockSpec((tile, hidden), lambda i, k, place: (i, 0)),
        ),
        out_shape=jax.ShapeDtypeStruct((tokens_dev, hidden), jnp.float32),
        compiler_params=pltpu.CompilerParams(vmem_limit_bytes=VMEM_LIMIT),
        cost_estimate=pl.CostEstimate(flops=EARLY_COST * hidden, bytes_accessed=0, transcendentals=0),
        name="early_part",
    )(place, grads, own, mate, near)


def pack_kernel(place, self_ref, other_ref, near_ref, packed_ref):
    inner = place[5] == 1

    @pl.when(inner)
    def _():
        packed_ref[...] = near_ref[...]

    @pl.when(jnp.logical_not(inner))
    def _():
        rows = packed_ref.shape[0] // 4
        count = packed_ref.shape[1] // UNIT
        for piece in range(4):
            source = self_ref if piece < 2 else other_ref
            for at in range(count):
                start = (piece % 2 * count + at) * rows
                packed_ref[piece * rows : (piece + 1) * rows, at * UNIT : (at + 1) * UNIT] = source[
                    start : start + rows, :
                ]


def pack(place, first, units, gates, near, near_first):
    tokens_dev = gates[0].shape[0]
    wide = 2 * tokens_dev
    gate = pl.BlockSpec((tokens_dev, UNIT), lambda i, place: (0, first + i))
    return pl.pallas_call(
        pack_kernel,
        grid_spec=pltpu.PrefetchScalarGridSpec(
            num_scalar_prefetch=1,
            grid=(units,),
            in_specs=[gate, gate, pl.BlockSpec((UNIT, wide), lambda i, place: (first - near_first + i, 0))],
            out_specs=pl.BlockSpec((UNIT, wide), lambda i, place: (i, 0)),
        ),
        out_shape=jax.ShapeDtypeStruct((units * UNIT, wide), near.dtype),
        compiler_params=pltpu.CompilerParams(vmem_limit_bytes=VMEM_LIMIT),
        cost_estimate=pl.CostEstimate(flops=0, bytes_accessed=1 << 20, transcendentals=0),
        name="pack",
    )(place, *gates, near)


def late_kernel(far_pieces, trade_pieces, per, place, *refs):
    refs = list(refs)
    take = lambda count: [refs.pop(0) for _ in range(count)]
    parts, grads, gate_refs, far_refs = take(2), take(2), take(2), take(far_pieces)
    guest_grad_ref, proj_ref, sum_ref, rest_ref = take(4)
    trade_refs = take(len(trade_pieces))
    packed_refs = take(sum(trade_pieces))
    (new_ref,) = refs
    inner = place[5] == 1
    rank = proj_ref.shape[0]
    step = pl.program_id(0)

    def project(upstream, gate, exact):
        gate = gate.astype(jnp.float32)
        up_grad = upstream * (gate / (1.0 + jnp.exp(-gate)))
        high = up_grad.astype(jnp.bfloat16)
        total = dot_nt(high, proj_ref[...])
        if exact:
            low = (up_grad - high.astype(jnp.float32)).astype(jnp.bfloat16)
            total = total + dot_nt(low, proj_ref[...])
        return total

    for group in range(2):

        @pl.when((step // per == group) & inner)
        def _(group=group):
            far = jnp.concatenate([ref[...] for ref in far_refs], axis=0)
            upstream = parts[group][...] + dot_nt(grads[group][0], far)
            new_ref[:, :rank] = sum_ref[:, :rank] + project(upstream, gate_refs[group][...], False)
            slabs = []
            for packed_ref in packed_refs:
                packed = packed_ref[...]
                slabs.append(
                    jnp.concatenate(
                        [packed[:, at : at + UNIT] for at in range(0, packed.shape[1], UNIT)], axis=0
                    )
                )
            guest = dot_nt(guest_grad_ref[0], far)
            new_ref[:, rank:] = sum_ref[:, rank:] + project(guest, jnp.concatenate(slabs, axis=1), True)

        @pl.when((step // per == group) & jnp.logical_not(inner))
        def _(group=group):
            weight = jnp.concatenate([ref[...] for ref in trade_refs], axis=0)
            weight = jnp.concatenate([weight, rest_ref[...]], axis=1)
            upstream = parts[group][...] + dot_nt(grads[group][0], weight)
            new_ref[:, :rank] = sum_ref[:, :rank] + project(upstream, gate_refs[group][...], True)
            new_ref[:, rank:] = sum_ref[:, rank:]


def late_part(place, first, base, parts, grads, fars, trades, rest, gates, guest_grads, proj_out, sums):
    tokens_dev, width = grads[0].shape[1:]
    tile = tokens_dev // 2
    per = tokens_dev // tile
    trade_pieces = tuple(trade.shape[0] // UNIT for trade in trades)
    units = sum(trade_pieces)
    wide = units * UNIT
    chunk, local = first // units, (first - base) // units
    trade_width = trades[0].shape[1]
    packed_rows = tile * UNIT // trade_width
    tiles = UNIT // packed_rows
    rank = proj_out.shape[0]
    at = (lambda i: jnp.minimum(i, per - 1), lambda i: jnp.maximum(i - per, 0))
    held = lambda array: pl.BlockSpec(array.shape, lambda i, place: (0, 0))
    summed = pl.BlockSpec((tile, 2 * rank), lambda i, place: ((i // per ^ place[0]) * per + i % per, 0))
    in_specs = (
        [pl.BlockSpec((tile, wide), lambda i, place, f=f: (f(i), local)) for f in at]
        + [pl.BlockSpec((1, tile, width), lambda i, place, f=f: (place[4], f(i), 0)) for f in at]
        + [pl.BlockSpec((tile, wide), lambda i, place, f=f: (f(i), chunk)) for f in at]
        + [held(far) for far in fars]
        + [
            pl.BlockSpec((1, tile, width), lambda i, place: (i // per ^ place[0], i % per, 0)),
            pl.BlockSpec((rank, wide), lambda i, place: (0, chunk)),
            summed,
            pl.BlockSpec((wide, rest.shape[1]), lambda i, place: (local, 0)),
        ]
        + [held(trade) for trade in trades]
        + [
            pl.BlockSpec((packed_rows, trade_width), lambda i, place, u=u: (u * tiles + i, 0))
            for pieces in trade_pieces
            for u in range(pieces)
        ]
    )
    return pl.pallas_call(
        functools.partial(late_kernel, len(fars), trade_pieces, per),
        grid_spec=pltpu.PrefetchScalarGridSpec(
            num_scalar_prefetch=1,
            grid=(2 * per,),
            in_specs=in_specs,
            out_specs=summed,
        ),
        out_shape=jax.ShapeDtypeStruct(sums.shape, jnp.float32),
        input_output_aliases={1 + 6 + len(fars) + 2: 0},
        compiler_params=pltpu.CompilerParams(vmem_limit_bytes=VMEM_LIMIT),
        cost_estimate=pl.CostEstimate(flops=LATE_COST, bytes_accessed=0, transcendentals=0),
        name="late_part",
    )(
        place, *parts, *grads, *gates, *fars, guest_grads, proj_out, sums, rest, *trades,
        *[trade for trade, pieces in zip(trades, trade_pieces) for _ in range(pieces)],
    )


def example_sums(counts, factors_in, factors_out):
    tok_rows = factors_in.shape[0]
    stop_at = jnp.cumsum(counts, dtype=jnp.int32)
    starts = stop_at - counts
    position = jnp.arange(tok_rows, dtype=jnp.int32)
    member = (
        (position[None, :] >= starts[:, None]) & (position[None, :] < stop_at[:, None])
    ).astype(jnp.float32)
    weighted = member[:, :, None] * factors_in[None, :, :]
    return jnp.einsum(
        "eti,tj->eij", weighted, factors_out, precision=lax.Precision.HIGHEST
    ).reshape(counts.shape[0], -1)


def own_fisher(example_grads):
    every = lax.all_gather(example_grads.astype(jnp.bfloat16), "dp", axis=0, tiled=True)
    fsdp_count = lax.axis_size("fsdp")
    own_rows = every.shape[1] // (lax.axis_size("dp") * fsdp_count)
    block = lax.axis_index("dp") * fsdp_count + lax.axis_index("fsdp")
    picked = lax.dynamic_slice_in_dim(every, block * own_rows, own_rows, 1)
    product = lax.dot_general(
        picked, every, (((0,), (0,)), ((), ())), preferred_element_type=jnp.float32
    )
    return product * (1.0 / every.shape[0])


def line_plan(acts, out_grad, gate_pre, down_weight, proj_in, proj_out, lengths):
    x, z, column = lax.axis_index("groups"), lax.axis_index("dp"), lax.axis_index("fsdp")
    inner = (z == 1) | (z == 2)
    near_block, far_block = jnp.where(z < 2, 2, 1), jnp.where(z < 2, 3, 0)
    place = jnp.stack(
        [x, z, z ^ 1, near_block, jnp.where(inner, far_block, near_block), inner.astype(jnp.int32)]
    ).astype(jnp.int32)
    tokens_dev, width = out_grad.shape
    hidden = down_weight.shape[0] // 2
    rank = proj_out.shape[0]
    cut = FIRST_UNITS * UNIT
    fsdp_count = lax.axis_size("fsdp")

    own_proj = lax.dynamic_slice_in_dim(proj_out, x * hidden, hidden, 1)
    own_first = lax.dynamic_slice_in_dim(down_weight, x * hidden, cut, 0)
    own_second = lax.dynamic_slice_in_dim(down_weight, x * hidden + cut, hidden - cut, 0)
    grads_self = lax.all_gather(out_grad, "fsdp", axis=0)
    grad_other = lax.ppermute(out_grad, "groups", SWAP)
    mate_first = lax.ppermute(own_first, "dp", MATES)
    near_first = lax.ppermute(own_first, "dp", ACROSS)
    gate_self = lax.dynamic_slice_in_dim(gate_pre, x * hidden, hidden, 1)
    gate_send = lax.dynamic_slice_in_dim(gate_pre, (1 - x) * hidden, hidden, 1)
    share_in = dot_nt(acts, proj_in)

    grads_self, grad_other, mate_first, near_first, gate_send, own_second, share_in = lax.optimization_barrier(
        (grads_self, grad_other, mate_first, near_first, gate_send, own_second, share_in)
    )
    mate_second = lax.ppermute(own_second, "dp", MATES)
    near_second = lax.ppermute(own_second, "dp", ACROSS)
    gate_other = lax.ppermute(gate_send, "groups", SWAP)
    grads_other = lax.all_gather(grad_other, "fsdp", axis=0)
    piece_rows = tokens_dev // fsdp_count
    piece = lax.dynamic_slice(grads_self, (far_block, column * piece_rows, 0), (1, piece_rows, width))[0]
    trade_width = 2 * tokens_dev
    lanes = width - trade_width
    slots = width // lanes
    slot_rows = cut // slots
    edge = near_first[:, trade_width:].reshape(slots, slot_rows, lanes).swapaxes(0, 1).reshape(slot_rows, width)
    edge = jnp.pad(edge, ((0, piece_rows - slot_rows), (0, 0)))
    piece = lax.ppermute(jnp.where(inner, edge, piece), "dp", MATES)
    far_start = lax.ppermute(mate_first[: LATE[0][1][0] * UNIT], "dp", ACROSS)
    part_self = early_part(place, grads_self, own_first, mate_first, near_first)

    mate_second, near_second, gate_other, piece, part_self, share_in, far_start = lax.optimization_barrier(
        (mate_second, near_second, gate_other, piece, part_self, share_in, far_start)
    )
    rest_first = piece[:slot_rows].reshape(slot_rows, slots, lanes).swapaxes(0, 1).reshape(cut, lanes)
    guest_grads = lax.all_gather(piece, ("groups", "fsdp"), axis=0, tiled=True).reshape(2, tokens_dev, width)
    factors_in = lax.psum(share_in, "fsdp")
    mates, nears = (mate_first, mate_second), (near_first, near_second)
    gates = (gate_self, gate_other)
    rests = (rest_first, lax.ppermute(near_second[:, trade_width:], "dp", OUTWARD))
    turn = place
    done = []
    parts_first, parts_second = [part_self], []
    for grads, share in ((grads_self, 1), (grads_other, 0), (grads_other, 1)):
        weights = (own_second, mate_second, near_second) if share else (own_first, mate_first, near_first)
        part = early_part(turn, grads, *weights)
        (parts_second if share else parts_first).append(part)
        done.append(part)
        turn, done[-1] = lax.optimization_barrier((place, part))
        (parts_second if share else parts_first)[-1] = done[-1]
    sums = jnp.zeros((2 * tokens_dev, 2 * rank), jnp.float32)

    def after(operand, order):
        return lax.optimization_barrier((operand, done[order - 1]))[0] if order else operand

    chunks = []
    first = 0
    for order, (units, far_pieces) in enumerate(LATE):
        half = int(first * UNIT >= cut)
        base = half * FIRST_UNITS
        fars = []
        at = first
        for count in far_pieces:
            if at:
                rows = after(mates[half][(at - base) * UNIT : (at - base + count) * UNIT], order)
                fars.append(lax.ppermute(rows, "dp", ACROSS))
            else:
                fars.append(far_start)
            at += count
        packed = pack(after(place, order), first, units, gates, nears[half], base)
        chunks.append((first, half, base, fars, lax.ppermute(packed, "dp", MATES)))
        first += units
    for first, half, base, fars, trade in chunks:
        if half and first == base:
            sums, factors_in = lax.optimization_barrier((sums, factors_in))
        sums = late_part(
            place, first, base, parts_second if half else parts_first, (grads_self, grads_other),
            fars, [trade], rests[half], gates, guest_grads, own_proj, sums,
        )

    spread = lax.all_to_all(
        sums.reshape(2 * fsdp_count, piece_rows, 2 * rank), ("groups", "fsdp"), split_axis=0, concat_axis=0
    ).sum(axis=0)
    mine = spread[:, :rank] + lax.ppermute(spread[:, rank:], "dp", OUTWARD)
    factors_out = lax.all_gather(mine, "fsdp", axis=0, tiled=True)
    return own_fisher(example_sums(lengths[0], factors_in, factors_out))


def ring_plan(acts, out_grad, gate_pre, down_weight, proj_in, proj_out, lengths):
    full_grad = lax.all_gather(out_grad, "fsdp", axis=1, tiled=True)
    upstream = dot_nt(full_grad, lax.all_gather(down_weight, "dp", axis=1, tiled=True))
    up_grad = (upstream * jax.nn.silu(gate_pre.astype(jnp.float32))).astype(jnp.bfloat16)
    rank_in = proj_in.shape[0]
    joined = lax.psum(jnp.concatenate([dot_nt(acts, proj_in), dot_nt(up_grad, proj_out)], axis=1), "fsdp")
    return own_fisher(example_sums(lengths[0], joined[:, :rank_in], joined[:, rank_in:]))


def solution(mesh):
    placed = (
        P(("groups", "dp"), "fsdp"),
        P(("groups", "dp"), "fsdp"),
        P(("groups", "dp"), "fsdp"),
        P("fsdp", "dp"),
        P(None, "fsdp"),
        P(None, "fsdp"),
        P(("groups", "dp"), None),
    )
    line = (mesh.shape["groups"], mesh.shape["dp"], mesh.shape["fsdp"]) == (2, 4, 4)
    return jax.shard_map(
        line_plan if line else ring_plan,
        mesh=mesh,
        in_specs=placed,
        out_specs=P(("groups", "dp", "fsdp"), None),
        check_vma=False,
    )
```

```python
import functools

import jax
import jax.numpy as jnp
from jax import lax
from jax.experimental import pallas as pl
from jax.experimental.pallas import tpu as pltpu
from jax.sharding import PartitionSpec as P

MATES = [(0, 1), (1, 0), (2, 3), (3, 2)]
ACROSS = [(1, 2), (2, 1)]
OUTWARD = [(1, 0), (2, 3)]
INWARD = [(0, 1), (3, 2)]
SWAP = [(0, 1), (1, 0)]
UNIT = 256
FIRST_UNITS = 4
LATE = ((4, (1, 3)), (2, (2,)), (1, (1,)))
EARLY_COST = 1 << 10
LATE_COST = 1 << 20
VMEM_LIMIT = 58 * 1024 * 1024


def dot_nt(left, right):
    return lax.dot_general(left, right, (((1,), (1,)), ((), ())), preferred_element_type=jnp.float32)


def early_kernel(place, grad_ref, own_ref, mate_ref, near_ref, part_ref):
    step = pl.program_id(1)

    @pl.when(step == 0)
    def _():
        part_ref[...] = dot_nt(grad_ref[0], own_ref[...])

    @pl.when(step == 1)
    def _():
        part_ref[...] += dot_nt(grad_ref[0], mate_ref[...])

    @pl.when(step == 2)
    def _():
        part_ref[...] += dot_nt(grad_ref[0], near_ref[...])


def early_part(place, grads, own, mate, near):
    hidden, width = own.shape
    tokens_dev = grads.shape[1]
    tile = tokens_dev // 2
    whole = pl.BlockSpec((hidden, width), lambda i, k, place: (0, 0), pipeline_mode=pl.Buffered(1))
    return pl.pallas_call(
        early_kernel,
        grid_spec=pltpu.PrefetchScalarGridSpec(
            num_scalar_prefetch=1,
            grid=(tokens_dev // tile, 3),
            in_specs=[pl.BlockSpec((1, tile, width), lambda i, k, place: (place[1 + k], i, 0)), whole, whole, whole],
            out_specs=pl.BlockSpec((tile, hidden), lambda i, k, place: (i, 0)),
        ),
        out_shape=jax.ShapeDtypeStruct((tokens_dev, hidden), jnp.float32),
        compiler_params=pltpu.CompilerParams(vmem_limit_bytes=VMEM_LIMIT),
        cost_estimate=pl.CostEstimate(flops=EARLY_COST * hidden, bytes_accessed=0, transcendentals=0),
        name="early_part",
    )(place, grads, own, mate, near)


def pack_kernel(place, self_ref, other_ref, near_ref, packed_ref):
    inner = place[5] == 1

    @pl.when(inner)
    def _():
        packed_ref[...] = near_ref[...]

    @pl.when(jnp.logical_not(inner))
    def _():
        rows, source_rows = packed_ref.shape[0] // 4, self_ref.shape[0]
        rest = packed_ref.shape[1] - 2 * source_rows
        if rest:
            packed_ref[:, 2 * source_rows :] = jnp.zeros((packed_ref.shape[0], rest), packed_ref.dtype)
        count = source_rows // (2 * rows)
        for piece in range(4):
            source = self_ref if piece < 2 else other_ref
            for at in range(count):
                start = (piece % 2 * count + at) * rows
                packed_ref[piece * rows : (piece + 1) * rows, at * UNIT : (at + 1) * UNIT] = source[
                    start : start + rows, :
                ]


def pack(place, first, units, gates, near, near_first, wide):
    tokens_dev = gates[0].shape[0]
    gate = pl.BlockSpec((tokens_dev, UNIT), lambda i, place: (0, first + i))
    return pl.pallas_call(
        pack_kernel,
        grid_spec=pltpu.PrefetchScalarGridSpec(
            num_scalar_prefetch=1,
            grid=(units,),
            in_specs=[gate, gate, pl.BlockSpec((UNIT, wide), lambda i, place: (first - near_first + i, 0))],
            out_specs=pl.BlockSpec((UNIT, wide), lambda i, place: (i, 0)),
        ),
        out_shape=jax.ShapeDtypeStruct((units * UNIT, wide), near.dtype),
        compiler_params=pltpu.CompilerParams(vmem_limit_bytes=VMEM_LIMIT),
        cost_estimate=pl.CostEstimate(flops=0, bytes_accessed=1 << 20, transcendentals=0),
        name="pack",
    )(place, *gates, near)


def late_kernel(far_pieces, rest_pieces, trade_pieces, per, place, *refs):
    refs = list(refs)
    take = lambda count: [refs.pop(0) for _ in range(count)]
    parts, grads, gate_refs, far_refs = take(2), take(2), take(2), take(far_pieces)
    guest_grad_ref, proj_ref, sum_ref = take(3)
    rest_refs = take(rest_pieces)
    trade_refs = take(len(trade_pieces))
    packed_refs = take(sum(trade_pieces))
    (new_ref,) = refs
    inner = place[5] == 1
    rank = proj_ref.shape[0]
    step = pl.program_id(0)

    def project(upstream, gate, exact):
        gate = gate.astype(jnp.float32)
        up_grad = upstream * (gate / (1.0 + jnp.exp(-gate)))
        high = up_grad.astype(jnp.bfloat16)
        total = dot_nt(high, proj_ref[...])
        if exact:
            low = (up_grad - high.astype(jnp.float32)).astype(jnp.bfloat16)
            total = total + dot_nt(low, proj_ref[...])
        return total

    for group in range(2):

        @pl.when((step // per == group) & inner)
        def _(group=group):
            far = jnp.concatenate([ref[...] for ref in far_refs], axis=0)
            upstream = parts[group][...] + dot_nt(grads[group][0], far)
            new_ref[:, :rank] = sum_ref[:, :rank] + project(upstream, gate_refs[group][...], False)
            slabs = []
            for packed_ref in packed_refs:
                packed = packed_ref[...]
                slabs.append(
                    jnp.concatenate(
                        [packed[:, at : at + UNIT] for at in range(0, packed.shape[1], UNIT)], axis=0
                    )
                )
            guest = dot_nt(guest_grad_ref[0], far)
            new_ref[:, rank:] = sum_ref[:, rank:] + project(guest, jnp.concatenate(slabs, axis=1), True)

        @pl.when((step // per == group) & jnp.logical_not(inner))
        def _(group=group):
            weight = jnp.concatenate([ref[...] for ref in trade_refs], axis=0)
            weight = jnp.concatenate([weight, *[ref[...] for ref in rest_refs]], axis=1)
            upstream = parts[group][...] + dot_nt(grads[group][0], weight)
            new_ref[:, :rank] = sum_ref[:, :rank] + project(upstream, gate_refs[group][...], True)
            new_ref[:, rank:] = sum_ref[:, rank:]


def late_part(place, first, base, parts, grads, fars, trades, rests, gates, guest_grads, proj_out, sums):
    tokens_dev, width = grads[0].shape[1:]
    tile = tokens_dev // 2
    per = tokens_dev // tile
    trade_pieces = tuple(trade.shape[0] // UNIT for trade in trades)
    units = sum(trade_pieces)
    wide = units * UNIT
    chunk, local = first // units, (first - base) // units
    trade_width = 2 * tokens_dev
    packed_rows = tile * UNIT // trade_width
    tiles = UNIT // packed_rows
    rank = proj_out.shape[0]
    at = (lambda i: jnp.minimum(i, per - 1), lambda i: jnp.maximum(i - per, 0))
    held = lambda array: pl.BlockSpec(array.shape, lambda i, place: (0, 0))
    summed = pl.BlockSpec((tile, 2 * rank), lambda i, place: ((i // per ^ place[0]) * per + i % per, 0))
    in_specs = (
        [pl.BlockSpec((tile, wide), lambda i, place, f=f: (f(i), local)) for f in at]
        + [pl.BlockSpec((1, tile, width), lambda i, place, f=f: (place[4], f(i), 0)) for f in at]
        + [pl.BlockSpec((tile, wide), lambda i, place, f=f: (f(i), chunk)) for f in at]
        + [held(far) for far in fars]
        + [
            pl.BlockSpec((1, tile, width), lambda i, place: (i // per ^ place[0], i % per, 0)),
            pl.BlockSpec((rank, wide), lambda i, place: (0, chunk)),
            summed,
        ]
        + [pl.BlockSpec((wide, rest.shape[1]), lambda i, place: (local, 0)) for rest in rests]
        + [held(trade) for trade in trades]
        + [
            pl.BlockSpec((packed_rows, trade_width), lambda i, place, u=u: (u * tiles + i, 0))
            for pieces in trade_pieces
            for u in range(pieces)
        ]
    )
    return pl.pallas_call(
        functools.partial(late_kernel, len(fars), len(rests), trade_pieces, per),
        grid_spec=pltpu.PrefetchScalarGridSpec(
            num_scalar_prefetch=1,
            grid=(2 * per,),
            in_specs=in_specs,
            out_specs=summed,
        ),
        out_shape=jax.ShapeDtypeStruct(sums.shape, jnp.float32),
        input_output_aliases={1 + 6 + len(fars) + 2: 0},
        compiler_params=pltpu.CompilerParams(vmem_limit_bytes=VMEM_LIMIT),
        cost_estimate=pl.CostEstimate(flops=LATE_COST, bytes_accessed=0, transcendentals=0),
        name="late_part",
    )(
        place, *parts, *grads, *gates, *fars, guest_grads, proj_out, sums, *rests, *trades,
        *[trade for trade, pieces in zip(trades, trade_pieces) for _ in range(pieces)],
    )


def example_sums(counts, factors_in, factors_out):
    tok_rows = factors_in.shape[0]
    stop_at = jnp.cumsum(counts, dtype=jnp.int32)
    starts = stop_at - counts
    position = jnp.arange(tok_rows, dtype=jnp.int32)
    member = (
        (position[None, :] >= starts[:, None]) & (position[None, :] < stop_at[:, None])
    ).astype(jnp.float32)
    weighted = member[:, :, None] * factors_in[None, :, :]
    return jnp.einsum(
        "eti,tj->eij", weighted, factors_out, precision=lax.Precision.HIGHEST
    ).reshape(counts.shape[0], -1)


def own_fisher(example_grads):
    every = lax.all_gather(example_grads.astype(jnp.bfloat16), "dp", axis=0, tiled=True)
    fsdp_count = lax.axis_size("fsdp")
    own_rows = every.shape[1] // (lax.axis_size("dp") * fsdp_count)
    block = lax.axis_index("dp") * fsdp_count + lax.axis_index("fsdp")
    picked = lax.dynamic_slice_in_dim(every, block * own_rows, own_rows, 1)
    product = lax.dot_general(
        picked, every, (((0,), (0,)), ((), ())), preferred_element_type=jnp.float32
    )
    return product * (1.0 / every.shape[0])


def line_plan(acts, out_grad, gate_pre, down_weight, proj_in, proj_out, lengths):
    x, z, column = lax.axis_index("groups"), lax.axis_index("dp"), lax.axis_index("fsdp")
    inner = (z == 1) | (z == 2)
    near_block, far_block = jnp.where(z < 2, 2, 1), jnp.where(z < 2, 3, 0)
    place = jnp.stack(
        [x, z, z ^ 1, near_block, jnp.where(inner, far_block, near_block), inner.astype(jnp.int32)]
    ).astype(jnp.int32)
    tokens_dev, width = out_grad.shape
    hidden = down_weight.shape[0] // 2
    rank = proj_out.shape[0]
    cut = FIRST_UNITS * UNIT
    fsdp_count = lax.axis_size("fsdp")

    own_proj = lax.dynamic_slice_in_dim(proj_out, x * hidden, hidden, 1)
    own_first = lax.dynamic_slice_in_dim(down_weight, x * hidden, cut, 0)
    own_second = lax.dynamic_slice_in_dim(down_weight, x * hidden + cut, hidden - cut, 0)
    grads_self = lax.all_gather(out_grad, "fsdp", axis=0)
    grad_other = lax.ppermute(out_grad, "groups", SWAP)
    mate_first = lax.ppermute(own_first, "dp", MATES)
    near_first = lax.ppermute(own_first, "dp", ACROSS)
    gate_self = lax.dynamic_slice_in_dim(gate_pre, x * hidden, hidden, 1)
    gate_send = lax.dynamic_slice_in_dim(gate_pre, (1 - x) * hidden, hidden, 1)
    share_in = dot_nt(acts, proj_in)

    grads_self, grad_other, mate_first, near_first, gate_send, own_second, share_in = lax.optimization_barrier(
        (grads_self, grad_other, mate_first, near_first, gate_send, own_second, share_in)
    )
    mate_second = lax.ppermute(own_second, "dp", MATES)
    near_second = lax.ppermute(own_second, "dp", ACROSS)
    gate_other = lax.ppermute(gate_send, "groups", SWAP)
    grads_other = lax.all_gather(grad_other, "fsdp", axis=0)
    piece_rows = tokens_dev // fsdp_count
    piece = lax.dynamic_slice(grads_self, (far_block, column * piece_rows, 0), (1, piece_rows, width))[0]
    trade_width = 2 * tokens_dev
    lanes = width - trade_width
    slots = width // lanes
    slot_rows = cut // slots
    edge = near_first[:, trade_width:].reshape(slots, slot_rows, lanes).swapaxes(0, 1).reshape(slot_rows, width)
    edge = jnp.pad(edge, ((0, piece_rows - slot_rows), (0, 0)))
    piece = lax.ppermute(jnp.where(inner, edge, piece), "dp", MATES)
    far_start = lax.ppermute(mate_first[: LATE[0][1][0] * UNIT], "dp", ACROSS)
    part_self = early_part(place, grads_self, own_first, mate_first, near_first)

    gates = (gate_self, gate_other)
    ready_far = mate_first[LATE[0][1][0] * UNIT : FIRST_UNITS * UNIT]
    ready_pack = pack(place, 0, FIRST_UNITS, gates, near_first, 0, trade_width)
    mate_second, near_second, piece, part_self, share_in, far_start, ready_far, ready_pack = lax.optimization_barrier(
        (mate_second, near_second, piece, part_self, share_in, far_start, ready_far, ready_pack)
    )
    rest_first = piece[:slot_rows].reshape(slot_rows, slots, lanes).swapaxes(0, 1).reshape(cut, lanes)
    guest_grads = lax.all_gather(piece, ("groups", "fsdp"), axis=0, tiled=True).reshape(2, tokens_dev, width)
    factors_in = lax.psum(share_in, "fsdp")
    mates, nears = (mate_first, mate_second), (near_first, near_second)
    rests = ([rest_first], [])
    turn = place
    done = []
    parts_first, parts_second = [part_self], []
    for grads, share in ((grads_self, 1), (grads_other, 0), (grads_other, 1)):
        weights = (own_second, mate_second, near_second) if share else (own_first, mate_first, near_first)
        part = early_part(turn, grads, *weights)
        (parts_second if share else parts_first).append(part)
        done.append(part)
        turn, done[-1] = lax.optimization_barrier((place, part))
        (parts_second if share else parts_first)[-1] = done[-1]
    sums = jnp.zeros((2 * tokens_dev, 2 * rank), jnp.float32)

    def after(operand, order):
        return lax.optimization_barrier((operand, done[2 * order - 2]))[0]

    chunks = []
    first = 0
    for order, (units, far_pieces) in enumerate(LATE):
        half = int(first * UNIT >= cut)
        base = half * FIRST_UNITS
        fars = []
        at = first
        for count in far_pieces:
            if at:
                rows = ready_far
                if order:
                    rows = after(mates[half][(at - base) * UNIT : (at - base + count) * UNIT], order)
                fars.append(lax.ppermute(rows, "dp", ACROSS))
            else:
                fars.append(far_start)
            at += count
        packed = pack(place, first, units, gates, nears[half], base, width) if order else ready_pack
        packed = after(packed, order) if order else packed
        chunks.append((first, half, base, fars, lax.ppermute(packed, "dp", MATES)))
        first += units
    for first, half, base, fars, trade in chunks:
        if half and first == base:
            sums, factors_in = lax.optimization_barrier((sums, factors_in))
        sums = late_part(
            place, first, base, parts_second if half else parts_first, (grads_self, grads_other),
            fars, [trade], rests[half], gates, guest_grads, own_proj, sums,
        )

    spread = lax.all_to_all(
        sums.reshape(2 * fsdp_count, piece_rows, 2 * rank), ("groups", "fsdp"), split_axis=0, concat_axis=0
    ).sum(axis=0)
    mine = spread[:, :rank] + lax.ppermute(spread[:, rank:], "dp", OUTWARD)
    factors_out = lax.all_gather(mine, "fsdp", axis=0, tiled=True)
    return own_fisher(example_sums(lengths[0], factors_in, factors_out))


def ring_plan(acts, out_grad, gate_pre, down_weight, proj_in, proj_out, lengths):
    full_grad = lax.all_gather(out_grad, "fsdp", axis=1, tiled=True)
    upstream = dot_nt(full_grad, lax.all_gather(down_weight, "dp", axis=1, tiled=True))
    up_grad = (upstream * jax.nn.silu(gate_pre.astype(jnp.float32))).astype(jnp.bfloat16)
    rank_in = proj_in.shape[0]
    joined = lax.psum(jnp.concatenate([dot_nt(acts, proj_in), dot_nt(up_grad, proj_out)], axis=1), "fsdp")
    return own_fisher(example_sums(lengths[0], joined[:, :rank_in], joined[:, rank_in:]))


def solution(mesh):
    placed = (
        P(("groups", "dp"), "fsdp"),
        P(("groups", "dp"), "fsdp"),
        P(("groups", "dp"), "fsdp"),
        P("fsdp", "dp"),
        P(None, "fsdp"),
        P(None, "fsdp"),
        P(("groups", "dp"), None),
    )
    line = (mesh.shape["groups"], mesh.shape["dp"], mesh.shape["fsdp"]) == (2, 4, 4)
    return jax.shard_map(
        line_plan if line else ring_plan,
        mesh=mesh,
        in_specs=placed,
        out_specs=P(("groups", "dp", "fsdp"), None),
        check_vma=False,
    )
```

```python
import functools

import jax
import jax.numpy as jnp
from jax import lax
from jax.experimental import pallas as pl
from jax.experimental.pallas import tpu as pltpu
from jax.sharding import PartitionSpec as P

MATES = [(0, 1), (1, 0), (2, 3), (3, 2)]
ACROSS = [(1, 2), (2, 1)]
OUTWARD = [(1, 0), (2, 3)]
INWARD = [(0, 1), (3, 2)]
SWAP = [(0, 1), (1, 0)]
UNIT = 256
FIRST_UNITS = 4
LATE = ((4, (192, 832)), (2, (512,)), (1, (256,)))
EARLY_COST = 1 << 10
LATE_COST = 1 << 20
VMEM_LIMIT = 58 * 1024 * 1024


def dot_nt(left, right):
    return lax.dot_general(left, right, (((1,), (1,)), ((), ())), preferred_element_type=jnp.float32)


def early_kernel(place, grad_ref, own_ref, mate_ref, near_ref, part_ref):
    step = pl.program_id(1)

    @pl.when(step == 0)
    def _():
        part_ref[...] = dot_nt(grad_ref[0], own_ref[...])

    @pl.when(step == 1)
    def _():
        part_ref[...] += dot_nt(grad_ref[0], mate_ref[...])

    @pl.when(step == 2)
    def _():
        part_ref[...] += dot_nt(grad_ref[0], near_ref[...])


def early_part(place, grads, own, mate, near):
    hidden, width = own.shape
    tokens_dev = grads.shape[1]
    tile = tokens_dev // 2
    whole = pl.BlockSpec((hidden, width), lambda i, k, place: (0, 0), pipeline_mode=pl.Buffered(1))
    return pl.pallas_call(
        early_kernel,
        grid_spec=pltpu.PrefetchScalarGridSpec(
            num_scalar_prefetch=1,
            grid=(tokens_dev // tile, 3),
            in_specs=[pl.BlockSpec((1, tile, width), lambda i, k, place: (place[1 + k], i, 0)), whole, whole, whole],
            out_specs=pl.BlockSpec((tile, hidden), lambda i, k, place: (i, 0)),
        ),
        out_shape=jax.ShapeDtypeStruct((tokens_dev, hidden), jnp.float32),
        compiler_params=pltpu.CompilerParams(vmem_limit_bytes=VMEM_LIMIT),
        cost_estimate=pl.CostEstimate(flops=EARLY_COST * hidden, bytes_accessed=0, transcendentals=0),
        name="early_part",
    )(place, grads, own, mate, near)


def pack_kernel(place, self_ref, other_ref, near_ref, packed_ref):
    inner = place[5] == 1

    @pl.when(inner)
    def _():
        packed_ref[...] = near_ref[...]

    @pl.when(jnp.logical_not(inner))
    def _():
        rows, source_rows = packed_ref.shape[0] // 4, self_ref.shape[0]
        rest = packed_ref.shape[1] - 2 * source_rows
        if rest:
            packed_ref[:, 2 * source_rows :] = jnp.zeros((packed_ref.shape[0], rest), packed_ref.dtype)
        count = source_rows // (2 * rows)
        for piece in range(4):
            source = self_ref if piece < 2 else other_ref
            for at in range(count):
                start = (piece % 2 * count + at) * rows
                packed_ref[piece * rows : (piece + 1) * rows, at * UNIT : (at + 1) * UNIT] = source[
                    start : start + rows, :
                ]


def pack(place, first, units, gates, near, near_first, wide):
    tokens_dev = gates[0].shape[0]
    gate = pl.BlockSpec((tokens_dev, UNIT), lambda i, place: (0, first + i))
    return pl.pallas_call(
        pack_kernel,
        grid_spec=pltpu.PrefetchScalarGridSpec(
            num_scalar_prefetch=1,
            grid=(units,),
            in_specs=[gate, gate, pl.BlockSpec((UNIT, wide), lambda i, place: (first - near_first + i, 0))],
            out_specs=pl.BlockSpec((UNIT, wide), lambda i, place: (i, 0)),
        ),
        out_shape=jax.ShapeDtypeStruct((units * UNIT, wide), near.dtype),
        compiler_params=pltpu.CompilerParams(vmem_limit_bytes=VMEM_LIMIT),
        cost_estimate=pl.CostEstimate(flops=0, bytes_accessed=1 << 20, transcendentals=0),
        name="pack",
    )(place, *gates, near)


def late_kernel(far_pieces, rest_pieces, trade_pieces, per, place, *refs):
    refs = list(refs)
    take = lambda count: [refs.pop(0) for _ in range(count)]
    parts, grads, gate_refs, far_refs = take(2), take(2), take(2), take(far_pieces)
    guest_grad_ref, proj_ref, sum_ref = take(3)
    rest_refs = take(rest_pieces)
    trade_refs = take(len(trade_pieces))
    packed_refs = take(sum(trade_pieces))
    (new_ref,) = refs
    inner = place[5] == 1
    rank = proj_ref.shape[0]
    step = pl.program_id(0)

    def project(upstream, gate, exact):
        half = 0.5 * gate.astype(jnp.float32)
        up_grad = upstream * (half + half * jnp.tanh(half))
        high = up_grad.astype(jnp.bfloat16)
        total = dot_nt(high, proj_ref[...])
        if exact:
            low = (up_grad - high.astype(jnp.float32)).astype(jnp.bfloat16)
            total = total + dot_nt(low, proj_ref[...])
        return total

    for group in range(2):

        @pl.when((step // per == group) & inner)
        def _(group=group):
            far = jnp.concatenate([ref[...] for ref in far_refs], axis=0)
            upstream = parts[group][...] + dot_nt(grads[group][0], far)
            new_ref[:, :rank] = sum_ref[:, :rank] + project(upstream, gate_refs[group][...], False)
            slabs = []
            for packed_ref in packed_refs:
                packed = packed_ref[...]
                slabs.append(
                    jnp.concatenate(
                        [packed[:, at : at + UNIT] for at in range(0, packed.shape[1], UNIT)], axis=0
                    )
                )
            guest = dot_nt(guest_grad_ref[0], far)
            new_ref[:, rank:] = sum_ref[:, rank:] + project(guest, jnp.concatenate(slabs, axis=1), True)

        @pl.when((step // per == group) & jnp.logical_not(inner))
        def _(group=group):
            weight = jnp.concatenate([ref[...] for ref in trade_refs], axis=0)
            weight = jnp.concatenate([weight, *[ref[...] for ref in rest_refs]], axis=1)
            upstream = parts[group][...] + dot_nt(grads[group][0], weight)
            new_ref[:, :rank] = sum_ref[:, :rank] + project(upstream, gate_refs[group][...], True)
            new_ref[:, rank:] = sum_ref[:, rank:]


def late_part(place, first, base, parts, grads, fars, trades, rests, gates, guest_grads, proj_out, sums):
    tokens_dev, width = grads[0].shape[1:]
    tile = tokens_dev // 2
    per = tokens_dev // tile
    trade_pieces = tuple(trade.shape[0] // UNIT for trade in trades)
    units = sum(trade_pieces)
    wide = units * UNIT
    chunk, local = first // units, (first - base) // units
    trade_width = 2 * tokens_dev
    packed_rows = tile * UNIT // trade_width
    tiles = UNIT // packed_rows
    rank = proj_out.shape[0]
    at = (lambda i: jnp.minimum(i, per - 1), lambda i: jnp.maximum(i - per, 0))
    held = lambda array: pl.BlockSpec(array.shape, lambda i, place: (0, 0))
    summed = pl.BlockSpec((tile, 2 * rank), lambda i, place: ((i // per ^ place[0]) * per + i % per, 0))
    in_specs = (
        [pl.BlockSpec((tile, wide), lambda i, place, f=f: (f(i), local)) for f in at]
        + [pl.BlockSpec((1, tile, width), lambda i, place, f=f: (place[4], f(i), 0)) for f in at]
        + [pl.BlockSpec((tile, wide), lambda i, place, f=f: (f(i), chunk)) for f in at]
        + [held(far) for far in fars]
        + [
            pl.BlockSpec((1, tile, width), lambda i, place: (i // per ^ place[0], i % per, 0)),
            pl.BlockSpec((rank, wide), lambda i, place: (0, chunk)),
            summed,
        ]
        + [pl.BlockSpec((wide, rest.shape[1]), lambda i, place: (local, 0)) for rest in rests]
        + [held(trade) for trade in trades]
        + [
            pl.BlockSpec((packed_rows, trade_width), lambda i, place, u=u: (u * tiles + i, 0))
            for pieces in trade_pieces
            for u in range(pieces)
        ]
    )
    return pl.pallas_call(
        functools.partial(late_kernel, len(fars), len(rests), trade_pieces, per),
        grid_spec=pltpu.PrefetchScalarGridSpec(
            num_scalar_prefetch=1,
            grid=(2 * per,),
            in_specs=in_specs,
            out_specs=summed,
        ),
        out_shape=jax.ShapeDtypeStruct(sums.shape, jnp.float32),
        input_output_aliases={1 + 6 + len(fars) + 2: 0},
        compiler_params=pltpu.CompilerParams(vmem_limit_bytes=VMEM_LIMIT),
        cost_estimate=pl.CostEstimate(flops=LATE_COST, bytes_accessed=0, transcendentals=0),
        name="late_part",
    )(
        place, *parts, *grads, *gates, *fars, guest_grads, proj_out, sums, *rests, *trades,
        *[trade for trade, pieces in zip(trades, trade_pieces) for _ in range(pieces)],
    )


def example_sums(counts, factors_in, factors_out):
    tok_rows = factors_in.shape[0]
    stop_at = jnp.cumsum(counts, dtype=jnp.int32)
    starts = stop_at - counts
    position = jnp.arange(tok_rows, dtype=jnp.int32)
    member = (
        (position[None, :] >= starts[:, None]) & (position[None, :] < stop_at[:, None])
    ).astype(jnp.float32)
    weighted = member[:, :, None] * factors_in[None, :, :]
    return jnp.einsum(
        "eti,tj->eij", weighted, factors_out, precision=lax.Precision.HIGHEST
    ).reshape(counts.shape[0], -1)


def own_fisher(example_grads):
    every = lax.all_gather(example_grads.astype(jnp.bfloat16), "dp", axis=0, tiled=True)
    fsdp_count = lax.axis_size("fsdp")
    own_rows = every.shape[1] // (lax.axis_size("dp") * fsdp_count)
    block = lax.axis_index("dp") * fsdp_count + lax.axis_index("fsdp")
    picked = lax.dynamic_slice_in_dim(every, block * own_rows, own_rows, 1)
    product = lax.dot_general(
        picked, every, (((0,), (0,)), ((), ())), preferred_element_type=jnp.float32
    )
    return product * (1.0 / every.shape[0])


def line_plan(acts, out_grad, gate_pre, down_weight, proj_in, proj_out, lengths):
    x, z, column = lax.axis_index("groups"), lax.axis_index("dp"), lax.axis_index("fsdp")
    inner = (z == 1) | (z == 2)
    near_block, far_block = jnp.where(z < 2, 2, 1), jnp.where(z < 2, 3, 0)
    place = jnp.stack(
        [x, z, z ^ 1, near_block, jnp.where(inner, far_block, near_block), inner.astype(jnp.int32)]
    ).astype(jnp.int32)
    tokens_dev, width = out_grad.shape
    hidden = down_weight.shape[0] // 2
    rank = proj_out.shape[0]
    cut = FIRST_UNITS * UNIT
    fsdp_count = lax.axis_size("fsdp")

    own_proj = lax.dynamic_slice_in_dim(proj_out, x * hidden, hidden, 1)
    own_first = lax.dynamic_slice_in_dim(down_weight, x * hidden, cut, 0)
    own_second = lax.dynamic_slice_in_dim(down_weight, x * hidden + cut, hidden - cut, 0)
    grads_self = lax.all_gather(out_grad, "fsdp", axis=0)
    grad_other = lax.ppermute(out_grad, "groups", SWAP)
    mate_first = lax.ppermute(own_first, "dp", MATES)
    near_first = lax.ppermute(own_first, "dp", ACROSS)
    gate_self = lax.dynamic_slice_in_dim(gate_pre, x * hidden, hidden, 1)
    gate_send = lax.dynamic_slice_in_dim(gate_pre, (1 - x) * hidden, hidden, 1)
    share_in = dot_nt(acts, proj_in)

    grads_self, grad_other, mate_first, near_first, gate_send, own_second, share_in = lax.optimization_barrier(
        (grads_self, grad_other, mate_first, near_first, gate_send, own_second, share_in)
    )
    mate_second = lax.ppermute(own_second, "dp", MATES)
    near_second = lax.ppermute(own_second, "dp", ACROSS)
    gate_other = lax.ppermute(gate_send, "groups", SWAP)
    grads_other = lax.all_gather(grad_other, "fsdp", axis=0)
    piece_rows = tokens_dev // fsdp_count
    piece = lax.dynamic_slice(grads_self, (far_block, column * piece_rows, 0), (1, piece_rows, width))[0]
    trade_width = 2 * tokens_dev
    lanes = width - trade_width
    slots = width // lanes
    slot_rows = cut // slots
    edge = near_first[:, trade_width:].reshape(slots, slot_rows, lanes).swapaxes(0, 1).reshape(slot_rows, width)
    edge = jnp.pad(edge, ((0, piece_rows - slot_rows), (0, 0)))
    piece = lax.ppermute(jnp.where(inner, edge, piece), "dp", MATES)
    far_start = lax.ppermute(mate_first[: LATE[0][1][0]], "dp", ACROSS)
    part_self = early_part(place, grads_self, own_first, mate_first, near_first)

    gates = (gate_self, gate_other)
    ready_far = mate_first[LATE[0][1][0] :]
    ready_pack = pack(place, 0, FIRST_UNITS, gates, near_first, 0, trade_width)
    mate_second, near_second, piece, part_self, share_in, far_start, ready_far, ready_pack = lax.optimization_barrier(
        (mate_second, near_second, piece, part_self, share_in, far_start, ready_far, ready_pack)
    )
    rest_first = piece[:slot_rows].reshape(slot_rows, slots, lanes).swapaxes(0, 1).reshape(cut, lanes)
    guest_grads = lax.all_gather(piece, ("groups", "fsdp"), axis=0, tiled=True).reshape(2, tokens_dev, width)
    factors_in = lax.psum(share_in, "fsdp")
    mates, nears = (mate_first, mate_second), (near_first, near_second)
    rests = ([rest_first], [])
    turn = place
    done = []
    parts_first, parts_second = [part_self], []
    for grads, share in ((grads_self, 1), (grads_other, 0), (grads_other, 1)):
        weights = (own_second, mate_second, near_second) if share else (own_first, mate_first, near_first)
        part = early_part(turn, grads, *weights)
        (parts_second if share else parts_first).append(part)
        done.append(part)
        turn, done[-1] = lax.optimization_barrier((place, part))
        (parts_second if share else parts_first)[-1] = done[-1]
    sums = jnp.zeros((2 * tokens_dev, 2 * rank), jnp.float32)

    def after(operand, order):
        return lax.optimization_barrier((operand, done[2 * order - 2]))[0]

    chunks = []
    first = 0
    for order, (units, far_pieces) in enumerate(LATE):
        half = int(first * UNIT >= cut)
        base = half * FIRST_UNITS
        fars = []
        at = first * UNIT
        for count in far_pieces:
            if at:
                rows = ready_far
                if order:
                    rows = after(mates[half][at - base * UNIT : at - base * UNIT + count], order)
                fars.append(lax.ppermute(rows, "dp", ACROSS))
            else:
                fars.append(far_start)
            at += count
        packed = pack(place, first, units, gates, nears[half], base, width) if order else ready_pack
        packed = after(packed, order) if order else packed
        chunks.append((first, half, base, fars, lax.ppermute(packed, "dp", MATES)))
        first += units
    for first, half, base, fars, trade in chunks:
        if half and first == base:
            sums, factors_in = lax.optimization_barrier((sums, factors_in))
        sums = late_part(
            place, first, base, parts_second if half else parts_first, (grads_self, grads_other),
            fars, [trade], rests[half], gates, guest_grads, own_proj, sums,
        )

    spread = lax.all_to_all(
        sums.reshape(2 * fsdp_count, piece_rows, 2 * rank), ("groups", "fsdp"), split_axis=0, concat_axis=0
    ).sum(axis=0)
    mine = spread[:, :rank] + lax.ppermute(spread[:, rank:], "dp", OUTWARD)
    factors_out = lax.all_gather(mine, "fsdp", axis=0, tiled=True)
    return own_fisher(example_sums(lengths[0], factors_in, factors_out))


def ring_plan(acts, out_grad, gate_pre, down_weight, proj_in, proj_out, lengths):
    full_grad = lax.all_gather(out_grad, "fsdp", axis=1, tiled=True)
    upstream = dot_nt(full_grad, lax.all_gather(down_weight, "dp", axis=1, tiled=True))
    up_grad = (upstream * jax.nn.silu(gate_pre.astype(jnp.float32))).astype(jnp.bfloat16)
    rank_in = proj_in.shape[0]
    joined = lax.psum(jnp.concatenate([dot_nt(acts, proj_in), dot_nt(up_grad, proj_out)], axis=1), "fsdp")
    return own_fisher(example_sums(lengths[0], joined[:, :rank_in], joined[:, rank_in:]))


def solution(mesh):
    placed = (
        P(("groups", "dp"), "fsdp"),
        P(("groups", "dp"), "fsdp"),
        P(("groups", "dp"), "fsdp"),
        P("fsdp", "dp"),
        P(None, "fsdp"),
        P(None, "fsdp"),
        P(("groups", "dp"), None),
    )
    line = (mesh.shape["groups"], mesh.shape["dp"], mesh.shape["fsdp"]) == (2, 4, 4)
    return jax.shard_map(
        line_plan if line else ring_plan,
        mesh=mesh,
        in_specs=placed,
        out_specs=P(("groups", "dp", "fsdp"), None),
        check_vma=False,
    )
```

```python
import functools

import jax
import jax.numpy as jnp
from jax import lax
from jax.experimental import pallas as pl
from jax.experimental.pallas import tpu as pltpu
from jax.sharding import PartitionSpec as P

MATES = [(0, 1), (1, 0), (2, 3), (3, 2)]
ACROSS = [(1, 2), (2, 1)]
OUTWARD = [(1, 0), (2, 3)]
INWARD = [(0, 1), (3, 2)]
SWAP = [(0, 1), (1, 0)]
UNIT = 256
FIRST_UNITS = 4
LATE = ((4, (192, 832)), (2, (512,)), (1, (256,)))
EARLY_COST = 1 << 10
LATE_COST = 1 << 20
VMEM_LIMIT = 58 * 1024 * 1024
EARLY_VMEM = 32 * 1024 * 1024


def dot_nt(left, right):
    return lax.dot_general(left, right, (((1,), (1,)), ((), ())), preferred_element_type=jnp.float32)


def early_kernel(place, grad_ref, own_ref, mate_ref, near_ref, part_ref):
    step = pl.program_id(1)

    @pl.when(step == 0)
    def _():
        part_ref[...] = dot_nt(grad_ref[0], own_ref[...])

    @pl.when(step == 1)
    def _():
        part_ref[...] += dot_nt(grad_ref[0], mate_ref[...])

    @pl.when(step == 2)
    def _():
        part_ref[...] += dot_nt(grad_ref[0], near_ref[...])


def early_part(place, grads, own, mate, near):
    hidden, width = own.shape
    tokens_dev = grads.shape[1]
    tile = tokens_dev // 2
    whole = pl.BlockSpec((hidden, width), lambda i, k, place: (0, 0), pipeline_mode=pl.Buffered(1))
    return pl.pallas_call(
        early_kernel,
        grid_spec=pltpu.PrefetchScalarGridSpec(
            num_scalar_prefetch=1,
            grid=(tokens_dev // tile, 3),
            in_specs=[pl.BlockSpec((1, tile, width), lambda i, k, place: (place[1 + k], i, 0)), whole, whole, whole],
            out_specs=pl.BlockSpec((tile, hidden), lambda i, k, place: (i, 0)),
        ),
        out_shape=jax.ShapeDtypeStruct((tokens_dev, hidden), jnp.float32),
        compiler_params=pltpu.CompilerParams(vmem_limit_bytes=EARLY_VMEM),
        cost_estimate=pl.CostEstimate(flops=EARLY_COST * hidden, bytes_accessed=0, transcendentals=0),
        name="early_part",
    )(place, grads, own, mate, near)


def pack_kernel(place, self_ref, other_ref, near_ref, packed_ref):
    inner = place[5] == 1

    @pl.when(inner)
    def _():
        packed_ref[...] = near_ref[...]

    @pl.when(jnp.logical_not(inner))
    def _():
        rows, source_rows = packed_ref.shape[0] // 4, self_ref.shape[0]
        rest = packed_ref.shape[1] - 2 * source_rows
        if rest:
            packed_ref[:, 2 * source_rows :] = jnp.zeros((packed_ref.shape[0], rest), packed_ref.dtype)
        count = source_rows // (2 * rows)
        for piece in range(4):
            source = self_ref if piece < 2 else other_ref
            for at in range(count):
                start = (piece % 2 * count + at) * rows
                packed_ref[piece * rows : (piece + 1) * rows, at * UNIT : (at + 1) * UNIT] = source[
                    start : start + rows, :
                ]


def pack(place, first, units, gates, near, near_first, wide):
    tokens_dev = gates[0].shape[0]
    gate = pl.BlockSpec((tokens_dev, UNIT), lambda i, place: (0, first + i))
    return pl.pallas_call(
        pack_kernel,
        grid_spec=pltpu.PrefetchScalarGridSpec(
            num_scalar_prefetch=1,
            grid=(units,),
            in_specs=[gate, gate, pl.BlockSpec((UNIT, wide), lambda i, place: (first - near_first + i, 0))],
            out_specs=pl.BlockSpec((UNIT, wide), lambda i, place: (i, 0)),
        ),
        out_shape=jax.ShapeDtypeStruct((units * UNIT, wide), near.dtype),
        compiler_params=pltpu.CompilerParams(vmem_limit_bytes=EARLY_VMEM),
        cost_estimate=pl.CostEstimate(flops=0, bytes_accessed=1 << 20, transcendentals=0),
        name="pack",
    )(place, *gates, near)


def late_kernel(far_pieces, rest_pieces, trade_pieces, per, place, *refs):
    refs = list(refs)
    take = lambda count: [refs.pop(0) for _ in range(count)]
    parts, grads, gate_refs, far_refs = take(2), take(2), take(2), take(far_pieces)
    guest_grad_ref, proj_ref, sum_ref = take(3)
    rest_refs = take(rest_pieces)
    trade_refs = take(len(trade_pieces))
    packed_refs = take(sum(trade_pieces))
    (new_ref,) = refs
    inner = place[5] == 1
    rank = proj_ref.shape[0]
    step = pl.program_id(0)

    def project(upstream, gate, exact):
        half = 0.5 * gate.astype(jnp.float32)
        up_grad = upstream * (half + half * jnp.tanh(half))
        high = up_grad.astype(jnp.bfloat16)
        total = dot_nt(high, proj_ref[...])
        if exact:
            low = (up_grad - high.astype(jnp.float32)).astype(jnp.bfloat16)
            total = total + dot_nt(low, proj_ref[...])
        return total

    for group in range(2):

        @pl.when((step // per == group) & inner)
        def _(group=group):
            far = jnp.concatenate([ref[...] for ref in far_refs], axis=0)
            upstream = parts[group][...] + dot_nt(grads[group][0], far)
            new_ref[:, :rank] = sum_ref[:, :rank] + project(upstream, gate_refs[group][...], False)
            slabs = []
            for packed_ref in packed_refs:
                packed = packed_ref[...]
                slabs.append(
                    jnp.concatenate(
                        [packed[:, at : at + UNIT] for at in range(0, packed.shape[1], UNIT)], axis=0
                    )
                )
            guest = dot_nt(guest_grad_ref[0], far)
            new_ref[:, rank:] = sum_ref[:, rank:] + project(guest, jnp.concatenate(slabs, axis=1), True)

        @pl.when((step // per == group) & jnp.logical_not(inner))
        def _(group=group):
            weight = jnp.concatenate([ref[...] for ref in trade_refs], axis=0)
            weight = jnp.concatenate([weight, *[ref[...] for ref in rest_refs]], axis=1)
            upstream = parts[group][...] + dot_nt(grads[group][0], weight)
            new_ref[:, :rank] = sum_ref[:, :rank] + project(upstream, gate_refs[group][...], True)
            new_ref[:, rank:] = sum_ref[:, rank:]


def late_part(place, first, base, parts, grads, fars, trades, rests, gates, guest_grads, proj_out, sums):
    tokens_dev, width = grads[0].shape[1:]
    tile = tokens_dev // 2
    per = tokens_dev // tile
    trade_pieces = tuple(trade.shape[0] // UNIT for trade in trades)
    units = sum(trade_pieces)
    wide = units * UNIT
    chunk, local = first // units, (first - base) // units
    trade_width = 2 * tokens_dev
    packed_rows = tile * UNIT // trade_width
    tiles = UNIT // packed_rows
    rank = proj_out.shape[0]
    at = (lambda i: jnp.minimum(i, per - 1), lambda i: jnp.maximum(i - per, 0))
    held = lambda array: pl.BlockSpec(array.shape, lambda i, place: (0, 0))
    summed = pl.BlockSpec((tile, 2 * rank), lambda i, place: ((i // per ^ place[0]) * per + i % per, 0))
    in_specs = (
        [pl.BlockSpec((tile, wide), lambda i, place, f=f: (f(i), local)) for f in at]
        + [pl.BlockSpec((1, tile, width), lambda i, place, f=f: (place[4], f(i), 0)) for f in at]
        + [pl.BlockSpec((tile, wide), lambda i, place, f=f: (f(i), chunk)) for f in at]
        + [held(far) for far in fars]
        + [
            pl.BlockSpec((1, tile, width), lambda i, place: (i // per ^ place[0], i % per, 0)),
            pl.BlockSpec((rank, wide), lambda i, place: (0, chunk)),
            summed,
        ]
        + [pl.BlockSpec((wide, rest.shape[1]), lambda i, place: (local, 0)) for rest in rests]
        + [held(trade) for trade in trades]
        + [
            pl.BlockSpec((packed_rows, trade_width), lambda i, place, u=u: (u * tiles + i, 0))
            for pieces in trade_pieces
            for u in range(pieces)
        ]
    )
    return pl.pallas_call(
        functools.partial(late_kernel, len(fars), len(rests), trade_pieces, per),
        grid_spec=pltpu.PrefetchScalarGridSpec(
            num_scalar_prefetch=1,
            grid=(2 * per,),
            in_specs=in_specs,
            out_specs=summed,
        ),
        out_shape=jax.ShapeDtypeStruct(sums.shape, jnp.float32),
        input_output_aliases={1 + 6 + len(fars) + 2: 0},
        compiler_params=pltpu.CompilerParams(vmem_limit_bytes=VMEM_LIMIT),
        cost_estimate=pl.CostEstimate(flops=LATE_COST, bytes_accessed=0, transcendentals=0),
        name="late_part",
    )(
        place, *parts, *grads, *gates, *fars, guest_grads, proj_out, sums, *rests, *trades,
        *[trade for trade, pieces in zip(trades, trade_pieces) for _ in range(pieces)],
    )


def example_sums(counts, factors_in, factors_out):
    tok_rows = factors_in.shape[0]
    stop_at = jnp.cumsum(counts, dtype=jnp.int32)
    starts = stop_at - counts
    position = jnp.arange(tok_rows, dtype=jnp.int32)
    member = (
        (position[None, :] >= starts[:, None]) & (position[None, :] < stop_at[:, None])
    ).astype(jnp.float32)
    weighted = member[:, :, None] * factors_in[None, :, :]
    return jnp.einsum(
        "eti,tj->eij", weighted, factors_out, precision=lax.Precision.HIGHEST
    ).reshape(counts.shape[0], -1)


def own_fisher(example_grads):
    every = lax.all_gather(example_grads.astype(jnp.bfloat16), "dp", axis=0, tiled=True)
    fsdp_count = lax.axis_size("fsdp")
    own_rows = every.shape[1] // (lax.axis_size("dp") * fsdp_count)
    block = lax.axis_index("dp") * fsdp_count + lax.axis_index("fsdp")
    picked = lax.dynamic_slice_in_dim(every, block * own_rows, own_rows, 1)
    product = lax.dot_general(
        picked, every, (((0,), (0,)), ((), ())), preferred_element_type=jnp.float32
    )
    return product * (1.0 / every.shape[0])


def line_plan(acts, out_grad, gate_pre, down_weight, proj_in, proj_out, lengths):
    x, z, column = lax.axis_index("groups"), lax.axis_index("dp"), lax.axis_index("fsdp")
    inner = (z == 1) | (z == 2)
    near_block, far_block = jnp.where(z < 2, 2, 1), jnp.where(z < 2, 3, 0)
    place = jnp.stack(
        [x, z, z ^ 1, near_block, jnp.where(inner, far_block, near_block), inner.astype(jnp.int32)]
    ).astype(jnp.int32)
    tokens_dev, width = out_grad.shape
    hidden = down_weight.shape[0] // 2
    rank = proj_out.shape[0]
    cut = FIRST_UNITS * UNIT
    fsdp_count = lax.axis_size("fsdp")

    own_proj = lax.dynamic_slice_in_dim(proj_out, x * hidden, hidden, 1)
    own_first = lax.dynamic_slice_in_dim(down_weight, x * hidden, cut, 0)
    own_second = lax.dynamic_slice_in_dim(down_weight, x * hidden + cut, hidden - cut, 0)
    grads_self = lax.all_gather(out_grad, "fsdp", axis=0)
    grad_other = lax.ppermute(out_grad, "groups", SWAP)
    mate_first = lax.ppermute(own_first, "dp", MATES)
    near_first = lax.ppermute(own_first, "dp", ACROSS)
    gate_self = lax.dynamic_slice_in_dim(gate_pre, x * hidden, hidden, 1)
    gate_send = lax.dynamic_slice_in_dim(gate_pre, (1 - x) * hidden, hidden, 1)
    share_in = dot_nt(acts, proj_in)

    grads_self, grad_other, mate_first, near_first, gate_send, own_second, share_in = lax.optimization_barrier(
        (grads_self, grad_other, mate_first, near_first, gate_send, own_second, share_in)
    )
    mate_second = lax.ppermute(own_second, "dp", MATES)
    near_second = lax.ppermute(own_second, "dp", ACROSS)
    gate_other = lax.ppermute(gate_send, "groups", SWAP)
    grads_other = lax.all_gather(grad_other, "fsdp", axis=0)
    piece_rows = tokens_dev // fsdp_count
    piece = lax.dynamic_slice(grads_self, (far_block, column * piece_rows, 0), (1, piece_rows, width))[0]
    trade_width = 2 * tokens_dev
    lanes = width - trade_width
    slots = width // lanes
    slot_rows = cut // slots
    edge = near_first[:, trade_width:].reshape(slots, slot_rows, lanes).swapaxes(0, 1).reshape(slot_rows, width)
    edge = jnp.pad(edge, ((0, piece_rows - slot_rows), (0, 0)))
    piece = lax.ppermute(jnp.where(inner, edge, piece), "dp", MATES)
    far_start = lax.ppermute(mate_first[: LATE[0][1][0]], "dp", ACROSS)
    part_self = early_part(place, grads_self, own_first, mate_first, near_first)

    gates = (gate_self, gate_other)
    ready_far = mate_first[LATE[0][1][0] :]
    ready_pack = pack(place, 0, FIRST_UNITS, gates, near_first, 0, trade_width)
    mate_second, near_second, piece, part_self, share_in, far_start, ready_far, ready_pack = lax.optimization_barrier(
        (mate_second, near_second, piece, part_self, share_in, far_start, ready_far, ready_pack)
    )
    rest_first = piece[:slot_rows].reshape(slot_rows, slots, lanes).swapaxes(0, 1).reshape(cut, lanes)
    guest_grads = lax.all_gather(piece, ("groups", "fsdp"), axis=0, tiled=True).reshape(2, tokens_dev, width)
    factors_in = lax.psum(share_in, "fsdp")
    mates, nears = (mate_first, mate_second), (near_first, near_second)
    rests = ([rest_first], [])
    turn = place
    done = []
    parts_first, parts_second = [part_self], []
    for grads, share in ((grads_self, 1), (grads_other, 0), (grads_other, 1)):
        weights = (own_second, mate_second, near_second) if share else (own_first, mate_first, near_first)
        part = early_part(turn, grads, *weights)
        (parts_second if share else parts_first).append(part)
        done.append(part)
        turn, done[-1] = lax.optimization_barrier((place, part))
        (parts_second if share else parts_first)[-1] = done[-1]
    sums = jnp.zeros((2 * tokens_dev, 2 * rank), jnp.float32)

    def after(operand, order):
        return lax.optimization_barrier((operand, done[2 * order - 2]))[0]

    chunks = []
    first = 0
    for order, (units, far_pieces) in enumerate(LATE):
        half = int(first * UNIT >= cut)
        base = half * FIRST_UNITS
        fars = []
        at = first * UNIT
        for count in far_pieces:
            if at:
                rows = ready_far
                if order:
                    rows = after(mates[half][at - base * UNIT : at - base * UNIT + count], order)
                fars.append(lax.ppermute(rows, "dp", ACROSS))
            else:
                fars.append(far_start)
            at += count
        packed = pack(place, first, units, gates, nears[half], base, width) if order else ready_pack
        packed = after(packed, order) if order else packed
        chunks.append((first, half, base, fars, lax.ppermute(packed, "dp", MATES)))
        first += units
    for first, half, base, fars, trade in chunks:
        if half and first == base:
            sums, factors_in = lax.optimization_barrier((sums, factors_in))
        sums = late_part(
            place, first, base, parts_second if half else parts_first, (grads_self, grads_other),
            fars, [trade], rests[half], gates, guest_grads, own_proj, sums,
        )

    spread = lax.all_to_all(
        sums.reshape(2 * fsdp_count, piece_rows, 2 * rank), ("groups", "fsdp"), split_axis=0, concat_axis=0
    ).sum(axis=0)
    mine = spread[:, :rank] + lax.ppermute(spread[:, rank:], "dp", OUTWARD)
    factors_out = lax.all_gather(mine, "fsdp", axis=0, tiled=True)
    return own_fisher(example_sums(lengths[0], factors_in, factors_out))


def ring_plan(acts, out_grad, gate_pre, down_weight, proj_in, proj_out, lengths):
    full_grad = lax.all_gather(out_grad, "fsdp", axis=1, tiled=True)
    upstream = dot_nt(full_grad, lax.all_gather(down_weight, "dp", axis=1, tiled=True))
    up_grad = (upstream * jax.nn.silu(gate_pre.astype(jnp.float32))).astype(jnp.bfloat16)
    rank_in = proj_in.shape[0]
    joined = lax.psum(jnp.concatenate([dot_nt(acts, proj_in), dot_nt(up_grad, proj_out)], axis=1), "fsdp")
    return own_fisher(example_sums(lengths[0], joined[:, :rank_in], joined[:, rank_in:]))


def solution(mesh):
    placed = (
        P(("groups", "dp"), "fsdp"),
        P(("groups", "dp"), "fsdp"),
        P(("groups", "dp"), "fsdp"),
        P("fsdp", "dp"),
        P(None, "fsdp"),
        P(None, "fsdp"),
        P(("groups", "dp"), None),
    )
    line = (mesh.shape["groups"], mesh.shape["dp"], mesh.shape["fsdp"]) == (2, 4, 4)
    return jax.shard_map(
        line_plan if line else ring_plan,
        mesh=mesh,
        in_specs=placed,
        out_specs=P(("groups", "dp", "fsdp"), None),
        check_vma=False,
    )
```
